32 devices in a mesh: sec: 2 (over y), exp: 8 (over z, x), hid: 2 (over core).
Axes of the slice: x: 2, y: 2, z: 4, core: 2. Of those that a mesh axis runs over, the one named last changes fastest.
Arguments:
- tokens: bfloat16 [1024, 4096], P('exp', ('sec', 'hid')), may hold values from -1200 to 1200
- norm_gain: bfloat16 [4096], P(('sec', 'hid')), may hold values from 0.5 to 2
- route_weight: float32 [1024, 2], P('exp'), may hold values from 0.1 to 1
- block_experts: int32 [8, 2], replicated, may hold values from 0 to 7, all different within a row; in each aligned block of 8 rows (0 to 7, 8 to 15, ...) at most 4 rows name the same one
- w_gate: bfloat16 [2, 4096, 32768], P('sec', None, ('exp', 'hid')), may hold values from -0.09375 to 0.09375
- w_up: bfloat16 [2, 4096, 32768], P('sec', None, ('exp', 'hid')), may hold values from -0.09375 to 0.09375
- w_down: bfloat16 [2, 32768, 4096], P('sec', ('exp', 'hid')), may hold values from -0.0625 to 0.0625
Outputs:
- moe_out: bfloat16 [1024, 4096], P('exp', ('sec', 'hid'))
The draws below stay inside these ranges and needn't reach their ends.
Inputs may be any that keep to these rules, and one draw needn't show every extreme that they name: `block_experts`: each row names 2 different experts; no expert is named by more than 4 rows, a bound that some block reaches; every expert is named by some row.
All inputs are finite; a program needn't handle non-finite values.
Results may differ from the reference program's by a relative error of at most 0.018.
Values may be sent and summed in bfloat16 or wider, within the bound.
A program may use at most 128 MiB of HBM per device.

```python
import math
import jax
import jax.numpy as jnp
import numpy as np
from jax import lax

D = 4096
FF = 8192
EXPERTS = 8
TOP = 2
BLK = 128
BLOCKS = 8
TOKENS = 1024
MOST = 4
FFD = 2048
N_SEC = 2


def draw_tokens(key, part):
    key_rows = jax.random.fold_in(key, 11)
    key_cols = jax.random.fold_in(key, 12)
    key_base = jax.random.fold_in(key, 13)
    row_scale = jnp.exp(jax.random.uniform(key_rows, (TOKENS, 1), jnp.float32) * math.log(10.0))
    ramp = 1.0 + 2.0 * jnp.arange(D, dtype=jnp.float32)[None, :] / (D - 1)
    col_scale = jnp.exp(jax.random.uniform(key_cols, (1, D), jnp.float32) * math.log(10.0)) * ramp
    base_vals = jax.random.truncated_normal(key_base, -4.0, 4.0, (TOKENS, D), jnp.float32)
    return (row_scale * col_scale * base_vals).astype(jnp.bfloat16)


def block_scale(key, dims, shards, smallest, largest):
    gain, own = 1.0, jax.random.fold_in(key, 6)
    for position, parts in shards:
        steps = jnp.exp(jax.random.uniform(jax.random.fold_in(own, position), (parts,), jnp.float32, smallest / len(shards), largest / len(shards)))
        gain = gain * jnp.repeat(steps, dims[position] // parts).reshape([-1 if axis == position else 1 for axis in range(len(dims))])
    return gain


def routed_block(key, own, number, rows, number_of, top, reach, lean):
    sequence = jax.random.permutation(key, number_of)
    heavy_load, ordinary = portions_of(number_of, rows * top, reach, lean, True), portions_of(number_of, rows * top, reach, lean, False)
    places = jnp.arange(number_of)

    def named(sizes, rotation):
        used = int((sizes > 0).sum())
        fixed = max(1, used // 4)
        moved = fixed + (places - fixed + rotation * (used - fixed)) % max(1, number_of - fixed)
        return jnp.zeros((number_of,), jnp.int32).at[sequence[jnp.where(places < fixed, places, moved)]].set(jnp.asarray(sizes, jnp.int32))

    sizes = jnp.where(number % 4 == 0, named(heavy_load, number // 4), named(ordinary, number - number // 4 - 1))
    mixed = jax.random.permutation(jax.random.fold_in(own, 3), number_of)
    donor, taker = mixed[0:number_of // 2 * 2:2], mixed[1:number_of // 2 * 2:2]
    slack = jnp.minimum(sizes[donor] - 1, reach - sizes[taker]) // 2
    slack = jnp.where((donor == sequence[0]) | (taker == sequence[0]) | (sizes[taker] == 0), 0, jnp.maximum(slack, 0))
    moved = jax.random.randint(jax.random.fold_in(own, 4), (number_of // 2,), 0, 1 << 20) % (slack + 1)
    sizes = sizes.at[donor].add(-moved).at[taker].add(moved)
    labels = jnp.searchsorted(jnp.cumsum(sizes), jnp.arange(rows * top), side="right").astype(jnp.int32)
    table = labels.reshape(top, rows).T
    table = table[jax.random.permutation(jax.random.fold_in(own, 1), rows)]
    rotation = jax.random.randint(jax.random.fold_in(own, 2), (rows, 1), 0, top)
    return jnp.take_along_axis(table, (jnp.arange(top)[None, :] + rotation) % top, axis=1)


def portions_of(count, total, reach, lean, full):
    weights = [(1 << 20) // math.isqrt(rank ** lean) + 1 for rank in range(1, count + 1)]
    largest = reach if full else min(reach, max(-(-total // count), total * weights[0] // sum(weights)))
    least = 1 if total - largest >= count - 1 else 0
    counts, rest = [largest] + [least] * (count - 1), total - largest - least * (count - 1)
    while rest > 0:
        candidates = [i for i in range(1, count) if counts[i] < largest] or [i for i in range(1, count) if counts[i] < reach]
        pool, remaining = sum([weights[i] for i in candidates]), rest
        for i in candidates:
            more = min(reach - counts[i], max(1, remaining * weights[i] // pool), rest)
            counts[i] = counts[i] + more
            rest = rest - more
    return np.array(counts)


def scatter_about(rng, shape, width, reach, split=(), kind=jnp.bfloat16):
    values = width * jax.random.normal(rng, shape, jnp.float32)
    if split:
        values = values * block_scale(rng, shape, split, -0.22, 0.18)
    return jnp.clip(values, -reach, reach).astype(kind)


def setup_inputs(seed: int = 0) -> dict:
    key_list = jax.random.split(jax.random.key(seed), 8)
    tokens = draw_tokens(jax.random.fold_in(key_list[7], 71), 0)
    norm_gain = jnp.clip(jnp.exp(math.log(2.0) - 1.3862944 * jax.random.uniform(key_list[1], (D,), jnp.float32) ** block_scale(key_list[1], (D,), ((0, 4),), -0.2, 0.2)), 0.5, 2.0).astype(jnp.bfloat16)
    route_weight = jnp.clip(jnp.exp(math.log(1.0) - 2.3025851 * jax.random.uniform(key_list[2], (TOKENS, TOP), jnp.float32) ** block_scale(key_list[2], (TOKENS, TOP), ((0, 8),), -0.2, 0.2)), 0.1, 1.0)
    block_experts_keys = jax.random.split(jax.random.fold_in(key_list[3], 1), BLOCKS // BLOCKS)
    block_experts_turns = jax.random.permutation(jax.random.fold_in(key_list[3], 3), BLOCKS // BLOCKS)
    block_experts = jax.vmap(lambda own, number: routed_block(jax.random.fold_in(key_list[3], 2), own, number, BLOCKS, EXPERTS, TOP, MOST, 2))(block_experts_keys, block_experts_turns).reshape((BLOCKS, TOP))
    w_gate = scatter_about(key_list[4], (N_SEC, D, EXPERTS * FF // N_SEC), D ** -0.5, 0.09375, ((0, 2), (2, 16)))
    w_up = scatter_about(key_list[5], (N_SEC, D, EXPERTS * FF // N_SEC), D ** -0.5, 0.09375, ((0, 2), (2, 16)))
    w_down = scatter_about(key_list[6], (N_SEC, EXPERTS * FF // N_SEC, D), FF ** -0.5, 0.0625, ((0, 2), (1, 16)))
    return {"tokens": tokens, "norm_gain": norm_gain, "route_weight": route_weight, "block_experts": block_experts, "w_gate": w_gate, "w_up": w_up, "w_down": w_down}


def reference(tokens, norm_gain, route_weight, block_experts, w_gate, w_up, w_down):
    values = tokens.astype(jnp.float32)
    rms_value = jnp.sqrt(lax.optimization_barrier(jnp.mean(values * values, axis=1, keepdims=True)) + 1e-05)
    normed = (values * norm_gain.astype(jnp.float32) / rms_value).astype(jnp.bfloat16)
    slab_width = FF // N_SEC
    group_count = FF // FFD

    def advance(running, assignment):
        block_id = assignment // TOP
        which_pick = assignment % TOP
        expert_id = block_experts[block_id, which_pick]
        first_col = (expert_id * slab_width).astype(jnp.int32)
        gate_cols = jnp.concatenate([lax.dynamic_slice_in_dim(w_gate[section], first_col, slab_width, 1) for section in range(N_SEC)], axis=1)
        up_cols = jnp.concatenate([lax.dynamic_slice_in_dim(w_up[section], first_col, slab_width, 1) for section in range(N_SEC)], axis=1)
        down_rows = jnp.concatenate([lax.dynamic_slice_in_dim(w_down[section], first_col, slab_width, 0) for section in range(N_SEC)], axis=0)
        first_row = (block_id * BLK).astype(jnp.int32)
        block_rows = lax.dynamic_slice_in_dim(normed, first_row, BLK, 0)
        gate_acc = jnp.dot(block_rows, gate_cols, preferred_element_type=jnp.float32)
        up_acc = jnp.dot(block_rows, up_cols, preferred_element_type=jnp.float32)
        activated = (jax.nn.silu(gate_acc) * up_acc).astype(jnp.bfloat16)
        grouped = jnp.einsum('tgf,gfd->gtd', activated.reshape(BLK, group_count, FFD).astype(jnp.float32), down_rows.reshape(group_count, FFD, D).astype(jnp.float32))
        rounded = lax.optimization_barrier(grouped.astype(jnp.bfloat16)).astype(jnp.float32)
        summed = lax.optimization_barrier(jnp.sum(rounded, axis=0))
        weight_col = lax.dynamic_slice(route_weight, (first_row, which_pick.astype(jnp.int32)), (BLK, 1))
        current = lax.dynamic_slice_in_dim(running, first_row, BLK, 0)
        running = lax.dynamic_update_slice_in_dim(running, current + weight_col * summed, first_row, 0)
        return (running, None)
    running, unused = lax.scan(advance, jnp.zeros((TOKENS, D), jnp.float32), jnp.arange(BLOCKS * TOP, dtype=jnp.int32))
    return running.astype(jnp.bfloat16)
```

```python
import functools

import jax
import jax.numpy as jnp
from jax import lax
from jax.experimental import pallas as pl
from jax.experimental.pallas import tpu as pltpu
from jax.sharding import PartitionSpec as P

EXPERTS = 8
BLK = 128
MOST = 4
MESH = pl.DeviceIdType.MESH
EXTRA = 16


def greet(n, hid):
    e, s, h = lax.axis_index("exp"), lax.axis_index("sec"), lax.axis_index("hid")
    i, par = e // 2, e % 2
    barrier = pltpu.get_barrier_semaphore()
    for k in range(1, n):
        peer = lax.rem(i + k, n) * 2 + par
        pl.semaphore_signal(barrier, inc=1, device_id={"exp": peer}, device_id_type=MESH)
    pl.semaphore_signal(barrier, inc=1, device_id={"exp": i * 2 + 1 - par}, device_id_type=MESH)
    pl.semaphore_signal(barrier, inc=1, device_id={"sec": 1 - s}, device_id_type=MESH)
    for k in range(1, hid):
        pl.semaphore_signal(barrier, inc=1, device_id={"hid": lax.rem(h + k, hid)}, device_id_type=MESH)
    pl.semaphore_wait(barrier, (n - 1) + 1 + 1 + (hid - 1))
    return e, i, par, s, h


def remote(src, dst, sems, where, device):
    return pltpu.make_async_remote_copy(
        src_ref=src, dst_ref=dst, send_sem=sems[0].at[where], recv_sem=sems[1].at[where],
        device_id=device, device_id_type=MESH,
    )


def gather_kernel(n, hid, tok_ref, gain_ref, bos_ref, out_ref, gathered, full,
                  zs, zr, xs, xr, ys, yr, hs, hr, gs, gr):
    e, i, par, s, h = greet(n, hid)
    tl, width = tok_ref.shape
    slots = MOST * BLK

    def rows_of(index):
        return gathered.at[index * tl // BLK, pl.ds(pl.multiple_of(lax.rem(index * tl, BLK), tl), tl), :]

    mine = rows_of(e)
    mine[...] = tok_ref[...]
    pair = {"exp": i * 2 + 1 - par}
    far = []
    for k in range(1, n):
        c = remote(mine, mine, (zs, zr), k, {"exp": lax.rem(i + k, n) * 2 + par})
        c.start()
        far.append(c)
    near = [remote(mine, mine, (xs, xr), 0, pair)]
    near[0].start()
    for k in range(1, n):
        far[k - 1].wait_recv()
        got = rows_of(lax.rem(i - k + n, n) * 2 + par)
        c = remote(got, got, (xs, xr), k, pair)
        c.start()
        near.append(c)
    for c in near:
        c.wait_recv()

    me = s * hid + h
    over = (1 - s) * hid + h
    full[me, slots:, :] = jnp.broadcast_to(gain_ref[...], (EXTRA, width))
    parts = [pl.ds(k * BLK, BLK) for k in range(MOST)]
    parts[-1] = pl.ds((MOST - 1) * BLK, BLK + EXTRA)
    side, own, passed = [], [], []
    for k in range(MOST):
        full[me, k * BLK:(k + 1) * BLK, :] = gathered[bos_ref[k]]
        ref = full.at[me, parts[k], :]
        c = remote(ref, ref, (ys, yr), k, {"sec": 1 - s})
        c.start()
        side.append(c)
        for q in range(1, hid):
            c = remote(ref, ref, (hs, hr), k * hid + q, {"hid": lax.rem(h + q, hid)})
            c.start()
            own.append(c)
    for k in range(MOST):
        side[k].wait_recv()
        ref = full.at[over, parts[k], :]
        for q in range(1, hid):
            c = remote(ref, ref, (gs, gr), k * hid + q, {"hid": lax.rem(h + q, hid)})
            c.start()
            passed.append(c)
    for c in own + passed:
        c.wait_recv()
    groups = 2 * hid

    def norm(step, carry):
        rows = pl.ds(pl.multiple_of(step * 32, 32), 32)
        total = jnp.zeros((32, 1), jnp.float32)
        for j in range(groups):
            v = full[j, rows, :].astype(jnp.float32)
            total = total + jnp.sum(v * v, axis=1, keepdims=True)
        rms = jnp.sqrt(total / (groups * width) + 1e-05)
        for j in range(groups):
            v = full[j, rows, :].astype(jnp.float32)
            gain = full[j, slots:slots + EXTRA, :].astype(jnp.float32)[0:1, :]
            out_ref[rows, j * width:(j + 1) * width] = (v * gain / rms).astype(out_ref.dtype)
        return carry

    lax.fori_loop(0, slots // 32, norm, 0)
    for c in far + near + side + own + passed:
        c.wait_send()


def reduce_kernel(n, hid, term_ref, fac_ref, slot_ref, out_ref, hbuf, ysend, ybuf, red, spread,
                  psend, pbuf, qsend, qbuf, hs, hr, ys, yr, xs, xr, zs, zr):
    e, i, par, s, h = greet(n, hid)
    tl, width = out_ref.shape

    def cols(sec, at):
        return pl.ds(pl.multiple_of((sec * hid + at) * width, width), width)

    first = []
    for k in range(MOST):
        rows = pl.ds(k * BLK, BLK)
        for side in range(2):
            sec = (1 - s) if side == 0 else s
            for q in range(1, hid):
                at = lax.rem(h + q, hid)
                c = remote(term_ref.at[rows, cols(sec, at)], hbuf.at[side, q, rows, :], (hs, hr),
                           (k * 2 + side) * hid + q, {"hid": at})
                c.start()
                first.append(c)
    across = []
    where = 0
    for k in range(MOST):
        rows = pl.ds(k * BLK, BLK)
        for side in range(2):
            sec = (1 - s) if side == 0 else s
            total = term_ref[rows, cols(sec, h)].astype(jnp.float32)
            for q in range(1, hid):
                first[where].wait_recv()
                where += 1
                total = total + hbuf[side, q, rows, :].astype(jnp.float32)
            if side == 0:
                ysend[rows, :] = total.astype(ysend.dtype)
                c = remote(ysend.at[rows, :], ybuf.at[rows, :], (ys, yr), k, {"sec": 1 - s})
                c.start()
                across.append(c)
            else:
                red[k] = total
    for k in range(MOST):
        rows = pl.ds(k * BLK, BLK)
        across[k].wait_recv()
        red[k] = red[k] + ybuf[rows, :].astype(jnp.float32)
    for b in range(spread.shape[0]):
        spread[b] = red[slot_ref[b]] * fac_ref[b * BLK:(b + 1) * BLK, :]

    def part(dest):
        return spread[dest * tl // BLK, pl.ds(pl.multiple_of(lax.rem(dest * tl, BLK), tl), tl), :]

    order = [k for k in range(1, n)] + [0]
    near = {}
    for k in order:
        j = lax.rem(i + k, n)
        psend[k] = part(j * 2 + 1 - par).astype(psend.dtype)
        c = remote(psend.at[k], pbuf.at[k], (xs, xr), k, {"exp": i * 2 + 1 - par})
        c.start()
        near[k] = c
    far = []
    for k in order:
        j = lax.rem(i + k, n)
        mine = part(j * 2 + par)
        near[k].wait_recv()
        mine = mine + pbuf[k].astype(jnp.float32)
        if k:
            qsend[k] = mine.astype(qsend.dtype)
            c = remote(qsend.at[k], qbuf.at[k], (zs, zr), k, {"exp": j * 2 + par})
            c.start()
            far.append(c)
        else:
            total = mine
    for k in range(1, n):
        far[k - 1].wait_recv()
        total = total + qbuf[k].astype(jnp.float32)
    out_ref[...] = total.astype(out_ref.dtype)
    for c in first + across + list(near.values()) + far:
        c.wait_send()


def per_device(tokens, norm_gain, route_weight, block_experts, w_gate, w_up, w_down):
    exp_devices = lax.axis_size("exp")
    hid = lax.axis_size("hid")
    n = exp_devices // 2
    group_size = exp_devices // EXPERTS
    my_expert = lax.axis_index("exp") // group_size
    tl, width = tokens.shape
    total_rows = tl * exp_devices
    num_blocks = total_rows // BLK
    slots = MOST * BLK
    model = w_gate.shape[1]
    hit = jnp.any(block_experts == my_expert, axis=1)
    ids = jnp.arange(num_blocks, dtype=jnp.int32)
    earlier = (ids[None, :] < ids[:, None]) & hit[None, :]
    slot_of_block = jnp.sum(earlier.astype(jnp.int32), axis=1)
    match = hit[None, :] & (slot_of_block[None, :] == jnp.arange(MOST, dtype=jnp.int32)[:, None])
    block_of_slot = jnp.sum(jnp.where(match, ids[None, :], 0), axis=1).astype(jnp.int32)
    safe_slot = jnp.where(hit, slot_of_block, 0).astype(jnp.int32)

    vmem = pl.BlockSpec(memory_space=pltpu.VMEM)
    smem = pl.BlockSpec(memory_space=pltpu.SMEM)
    dma = pltpu.SemaphoreType.DMA
    bf = jnp.bfloat16
    normed = pl.pallas_call(
        functools.partial(gather_kernel, n, hid),
        out_shape=jax.ShapeDtypeStruct((slots, model), bf),
        in_specs=[vmem, vmem, smem],
        out_specs=vmem,
        scratch_shapes=[
            pltpu.VMEM((num_blocks, BLK, width), bf),
            pltpu.VMEM((2 * hid, slots + EXTRA, width), bf),
            dma((n,)), dma((n,)), dma((n,)), dma((n,)), dma((MOST,)), dma((MOST,)),
            dma((MOST * hid,)), dma((MOST * hid,)), dma((MOST * hid,)), dma((MOST * hid,)),
        ],
        compiler_params=pltpu.CompilerParams(
            collective_id=0, has_side_effects=True, vmem_limit_bytes=32 * 2**20),
    )(tokens, norm_gain.reshape(1, width), block_of_slot)

    weights = lax.all_gather(route_weight, "exp", axis=0, tiled=True)
    chosen = jnp.repeat(block_experts == my_expert, BLK, axis=0)
    factor = jnp.sum(jnp.where(chosen, weights, 0.0), axis=1, keepdims=True)

    gate = jnp.dot(normed, w_gate[0], preferred_element_type=jnp.float32)
    up = jnp.dot(normed, w_up[0], preferred_element_type=jnp.float32)
    act = (jax.nn.silu(gate) * up).astype(bf)
    terms = jnp.dot(act, w_down[0], preferred_element_type=jnp.float32).astype(bf)

    return pl.pallas_call(
        functools.partial(reduce_kernel, n, hid),
        out_shape=jax.ShapeDtypeStruct((tl, width), bf),
        in_specs=[vmem, vmem, smem],
        out_specs=vmem,
        scratch_shapes=[
            pltpu.VMEM((2, hid, slots, width), bf),
            pltpu.VMEM((slots, width), bf),
            pltpu.VMEM((slots, width), bf),
            pltpu.VMEM((MOST, BLK, width), jnp.float32),
            pltpu.VMEM((num_blocks, BLK, width), jnp.float32),
            pltpu.VMEM((n, tl, width), bf),
            pltpu.VMEM((n, tl, width), bf),
            pltpu.VMEM((n, tl, width), bf),
            pltpu.VMEM((n, tl, width), bf),
            dma((2 * MOST * hid,)), dma((2 * MOST * hid,)), dma((MOST,)), dma((MOST,)),
            dma((n,)), dma((n,)), dma((n,)), dma((n,)),
        ],
        compiler_params=pltpu.CompilerParams(
            collective_id=1, has_side_effects=True, vmem_limit_bytes=40 * 2**20),
    )(terms, factor, safe_slot)


def solution(mesh):
    return jax.shard_map(
        per_device,
        mesh=mesh,
        in_specs=(
            P("exp", ("sec", "hid")),
            P(("sec", "hid")),
            P("exp", None),
            P(),
            P("sec", None, ("exp", "hid")),
            P("sec", None, ("exp", "hid")),
            P("sec", ("exp", "hid"), None),
        ),
        out_specs=P("exp", ("sec", "hid")),
        check_vma=False,
    )
```

```python
import functools

import jax
import jax.numpy as jnp
from jax import lax
from jax.experimental import pallas as pl
from jax.experimental.pallas import tpu as pltpu
from jax.sharding import PartitionSpec as P

EXPERTS = 8
BLK = 128
MOST = 4
MESH = pl.DeviceIdType.MESH
EXTRA = 16


def greet(n, hid):
    e, s, h = lax.axis_index("exp"), lax.axis_index("sec"), lax.axis_index("hid")
    i, par = e // 2, e % 2
    barrier = pltpu.get_barrier_semaphore()
    for k in range(1, n):
        peer = lax.rem(i + k, n) * 2 + par
        pl.semaphore_signal(barrier, inc=1, device_id={"exp": peer}, device_id_type=MESH)
    pl.semaphore_signal(barrier, inc=1, device_id={"exp": i * 2 + 1 - par}, device_id_type=MESH)
    pl.semaphore_signal(barrier, inc=1, device_id={"sec": 1 - s}, device_id_type=MESH)
    for k in range(1, hid):
        pl.semaphore_signal(barrier, inc=1, device_id={"hid": lax.rem(h + k, hid)}, device_id_type=MESH)
    pl.semaphore_wait(barrier, (n - 1) + 1 + 1 + (hid - 1))
    return e, i, par, s, h


def remote(src, dst, sems, where, device):
    return pltpu.make_async_remote_copy(
        src_ref=src, dst_ref=dst, send_sem=sems[0].at[where], recv_sem=sems[1].at[where],
        device_id=device, device_id_type=MESH,
    )


def gather_kernel(n, hid, chunks, tok_ref, gain_ref, rw_ref, bos_ref, out_ref, rw_out, full, gw, *rest):
    gathered = rest[:chunks]
    zs, zr, xs, xr, ys, yr, hs, hr, gs, gr, ws, wr, vs, vr = rest[chunks:]
    e, i, par, s, h = greet(n, hid)
    tl = tok_ref.shape[0]
    half = full.shape[2]
    slots = MOST * BLK
    groups = full.shape[0]
    pair = {"exp": i * 2 + 1 - par}
    me = s * hid + h
    over = (1 - s) * hid + h
    parts = [pl.ds(k * BLK, BLK) for k in range(MOST)]
    parts[-1] = pl.ds((MOST - 1) * BLK, BLK + EXTRA)
    far, near, side, passed = {}, {}, {}, []

    def rows_of(c, index):
        return gathered[c].at[index * tl // BLK, pl.ds(pl.multiple_of(lax.rem(index * tl, BLK), tl), tl), :]

    def start(c):
        mine = rows_of(c, e)
        mine[...] = tok_ref[:, c * half:(c + 1) * half]
        for k in range(1, n):
            far[c, k] = remote(mine, mine, (zs, zr), c * n + k, {"exp": lax.rem(i + k, n) * 2 + par})
            far[c, k].start()
        near[c, 0] = remote(mine, mine, (xs, xr), c * n, pair)
        near[c, 0].start()

    def forward(c):
        for k in range(1, n):
            far[c, k].wait_recv()
            got = rows_of(c, lax.rem(i - k + n, n) * 2 + par)
            near[c, k] = remote(got, got, (xs, xr), c * n + k, pair)
            near[c, k].start()

    def pick(c):
        for k in range(n):
            near[c, k].wait_recv()
        spot = me * chunks + c
        full[spot, slots:, :] = jnp.broadcast_to(gain_ref[:, c * half:(c + 1) * half], (EXTRA, half))
        for k in range(MOST):
            full[spot, k * BLK:(k + 1) * BLK, :] = gathered[c][bos_ref[k]]
            ref = full.at[spot, parts[k], :]
            at = c * MOST + k
            side[c, k] = remote(ref, ref, (ys, yr), at, {"sec": 1 - s})
            side[c, k].start()
            for q in range(1, hid):
                copy = remote(ref, ref, (hs, hr), at * hid + q, {"hid": lax.rem(h + q, hid)})
                copy.start()
                passed.append(copy)

    def share(c):
        for k in range(MOST):
            side[c, k].wait_recv()
            ref = full.at[over * chunks + c, parts[k], :]
            for q in range(1, hid):
                copy = remote(ref, ref, (gs, gr), (c * MOST + k) * hid + q, {"hid": lax.rem(h + q, hid)})
                copy.start()
                passed.append(copy)

    gw[e] = rw_ref[...]
    wfar, wnear = [], [remote(gw.at[e], gw.at[e], (vs, vr), 0, pair)]
    start(0)
    for k in range(1, n):
        copy = remote(gw.at[e], gw.at[e], (ws, wr), k, {"exp": lax.rem(i + k, n) * 2 + par})
        copy.start()
        wfar.append(copy)
    wnear[0].start()
    for t in range(chunks + 2):
        if 0 <= t - 2:
            share(t - 2)
        if 0 <= t - 1 < chunks:
            pick(t - 1)
        if t < chunks:
            forward(t)
        if t + 1 < chunks:
            start(t + 1)
    for k in range(1, n):
        wfar[k - 1].wait_recv()
        got = gw.at[lax.rem(i - k + n, n) * 2 + par]
        copy = remote(got, got, (vs, vr), k, pair)
        copy.start()
        wnear.append(copy)
    for copy in passed:
        copy.wait_recv()

    def norm(step, carry):
        rows = pl.ds(pl.multiple_of(step * 32, 32), 32)
        total = jnp.zeros((32, 1), jnp.float32)
        for j in range(groups):
            v = full[j, rows, :].astype(jnp.float32)
            total = total + jnp.sum(v * v, axis=1, keepdims=True)
        rms = jnp.sqrt(total / (groups * half) + 1e-05)
        for j in range(groups):
            v = full[j, rows, :].astype(jnp.float32)
            gain = full[j, slots:slots + EXTRA, :].astype(jnp.float32)[0:1, :]
            out_ref[rows, j * half:(j + 1) * half] = (v * gain / rms).astype(out_ref.dtype)
        return carry

    lax.fori_loop(0, slots // 32, norm, 0)
    for copy in wnear:
        copy.wait_recv()
    rw_out[...] = gw[...]
    for copy in list(far.values()) + list(near.values()) + list(side.values()) + passed + wfar + wnear:
        copy.wait_send()


def ffn_kernel(first, tile, x_ref, gate_ref, up_ref, down_ref, out_ref, act):
    j = pl.program_id(0)

    @pl.when(j < first)
    def _():
        x = x_ref[...]
        gate = jnp.dot(x, gate_ref[0], preferred_element_type=jnp.float32)
        up = jnp.dot(x, up_ref[0], preferred_element_type=jnp.float32)
        vals = gate / (1.0 + jnp.exp(-gate)) * up
        act[:, pl.ds(pl.multiple_of(j * tile, tile), tile)] = vals.astype(act.dtype)

    @pl.when(j >= first)
    def _():
        out_ref[...] = jnp.dot(act[...], down_ref[0], preferred_element_type=jnp.float32).astype(out_ref.dtype)


def reduce_kernel(n, hid, term_ref, fac_ref, slot_ref, out_ref, hbuf, ysend, ybuf, red, spread,
                  psend, pbuf, qsend, qbuf, hs, hr, ys, yr, xs, xr, zs, zr):
    e, i, par, s, h = greet(n, hid)
    tl, width = out_ref.shape

    def cols(sec, at):
        return pl.ds(pl.multiple_of((sec * hid + at) * width, width), width)

    first = []
    for k in range(MOST):
        rows = pl.ds(k * BLK, BLK)
        for side in range(2):
            sec = (1 - s) if side == 0 else s
            for q in range(1, hid):
                at = lax.rem(h + q, hid)
                c = remote(term_ref.at[rows, cols(sec, at)], hbuf.at[side, q, rows, :], (hs, hr),
                           (k * 2 + side) * hid + q, {"hid": at})
                c.start()
                first.append(c)
    across = []
    where = 0
    for k in range(MOST):
        rows = pl.ds(k * BLK, BLK)
        for side in range(2):
            sec = (1 - s) if side == 0 else s
            total = term_ref[rows, cols(sec, h)].astype(jnp.float32)
            for q in range(1, hid):
                first[where].wait_recv()
                where += 1
                total = total + hbuf[side, q, rows, :].astype(jnp.float32)
            if side == 0:
                ysend[rows, :] = total.astype(ysend.dtype)
                c = remote(ysend.at[rows, :], ybuf.at[rows, :], (ys, yr), k, {"sec": 1 - s})
                c.start()
                across.append(c)
            else:
                red[k] = total
    for k in range(MOST):
        rows = pl.ds(k * BLK, BLK)
        across[k].wait_recv()
        red[k] = red[k] + ybuf[rows, :].astype(jnp.float32)
    for b in range(spread.shape[0]):
        spread[b] = red[slot_ref[b]] * fac_ref[b * BLK:(b + 1) * BLK, :]

    def part(dest):
        return spread[dest * tl // BLK, pl.ds(pl.multiple_of(lax.rem(dest * tl, BLK), tl), tl), :]

    order = [k for k in range(1, n)] + [0]
    near = {}
    for k in order:
        j = lax.rem(i + k, n)
        psend[k] = part(j * 2 + 1 - par).astype(psend.dtype)
        c = remote(psend.at[k], pbuf.at[k], (xs, xr), k, {"exp": i * 2 + 1 - par})
        c.start()
        near[k] = c
    far = []
    for k in order:
        j = lax.rem(i + k, n)
        mine = part(j * 2 + par)
        near[k].wait_recv()
        mine = mine + pbuf[k].astype(jnp.float32)
        if k:
            qsend[k] = mine.astype(qsend.dtype)
            c = remote(qsend.at[k], qbuf.at[k], (zs, zr), k, {"exp": j * 2 + par})
            c.start()
            far.append(c)
        else:
            total = mine
    for k in range(1, n):
        far[k - 1].wait_recv()
        total = total + qbuf[k].astype(jnp.float32)
    out_ref[...] = total.astype(out_ref.dtype)
    for c in first + across + list(near.values()) + far:
        c.wait_send()


def per_device(tokens, norm_gain, route_weight, block_experts, w_gate, w_up, w_down):
    exp_devices = lax.axis_size("exp")
    hid = lax.axis_size("hid")
    n = exp_devices // 2
    group_size = exp_devices // EXPERTS
    my_expert = lax.axis_index("exp") // group_size
    tl, width = tokens.shape
    total_rows = tl * exp_devices
    num_blocks = total_rows // BLK
    slots = MOST * BLK
    model = w_gate.shape[1]
    hit = jnp.any(block_experts == my_expert, axis=1)
    ids = jnp.arange(num_blocks, dtype=jnp.int32)
    earlier = (ids[None, :] < ids[:, None]) & hit[None, :]
    slot_of_block = jnp.sum(earlier.astype(jnp.int32), axis=1)
    match = hit[None, :] & (slot_of_block[None, :] == jnp.arange(MOST, dtype=jnp.int32)[:, None])
    block_of_slot = jnp.sum(jnp.where(match, ids[None, :], 0), axis=1).astype(jnp.int32)
    safe_slot = jnp.where(hit, slot_of_block, 0).astype(jnp.int32)

    vmem = pl.BlockSpec(memory_space=pltpu.VMEM)
    smem = pl.BlockSpec(memory_space=pltpu.SMEM)
    dma = pltpu.SemaphoreType.DMA
    bf = jnp.bfloat16
    chunks = 2 if width % 256 == 0 else 1
    half = width // chunks
    lanes = max(BLK, tl)
    packed = jnp.zeros((8, lanes), jnp.float32).at[:route_weight.shape[1], :tl].set(route_weight.T)
    normed, weights = pl.pallas_call(
        functools.partial(gather_kernel, n, hid, chunks),
        out_shape=(
            jax.ShapeDtypeStruct((slots, model), bf),
            jax.ShapeDtypeStruct((exp_devices, 8, lanes), jnp.float32),
        ),
        in_specs=[vmem, vmem, vmem, smem],
        out_specs=(vmem, vmem),
        scratch_shapes=[
            pltpu.VMEM((2 * hid * chunks, slots + EXTRA, half), bf),
            pltpu.VMEM((exp_devices, 8, lanes), jnp.float32),
            *[pltpu.VMEM((num_blocks, BLK, half), bf)] * chunks,
            *[dma((chunks * n,))] * 4,
            *[dma((chunks * MOST,))] * 2,
            *[dma((chunks * MOST * hid,))] * 4,
            *[dma((n,))] * 4,
        ],
        compiler_params=pltpu.CompilerParams(
            collective_id=0, has_side_effects=True, vmem_limit_bytes=32 * 2**20),
    )(tokens, norm_gain.reshape(1, width), packed, block_of_slot)

    weights = weights[:, :route_weight.shape[1], :tl].transpose(0, 2, 1).reshape(total_rows, -1)
    chosen = jnp.repeat(block_experts == my_expert, BLK, axis=0)
    factor = jnp.sum(jnp.where(chosen, weights, 0.0), axis=1, keepdims=True)

    units = w_gate.shape[2]
    tile = min(256, units)
    first = units // tile
    out_tile = min(512, model)
    flops = 6 * slots * model * units
    terms = pl.pallas_call(
        functools.partial(ffn_kernel, first, tile),
        grid=(first + model // out_tile,),
        out_shape=jax.ShapeDtypeStruct((slots, model), bf),
        in_specs=[
            pl.BlockSpec((slots, model), lambda j: (0, 0)),
            pl.BlockSpec((1, model, tile), lambda j: (0, 0, jnp.minimum(j, first - 1))),
            pl.BlockSpec((1, model, tile), lambda j: (0, 0, jnp.minimum(j, first - 1))),
            pl.BlockSpec((1, units, out_tile), lambda j: (0, 0, jnp.maximum(j - first, 0))),
        ],
        out_specs=pl.BlockSpec((slots, out_tile), lambda j: (0, jnp.maximum(j - first, 0))),
        scratch_shapes=[pltpu.VMEM((slots, units), bf)],
        compiler_params=pltpu.CompilerParams(vmem_limit_bytes=40 * 2**20),
        cost_estimate=pl.CostEstimate(
            flops=flops, bytes_accessed=6 * model * units, transcendentals=slots * units),
    )(normed, w_gate, w_up, w_down)

    return pl.pallas_call(
        functools.partial(reduce_kernel, n, hid),
        out_shape=jax.ShapeDtypeStruct((tl, width), bf),
        in_specs=[vmem, vmem, smem],
        out_specs=vmem,
        scratch_shapes=[
            pltpu.VMEM((2, hid, slots, width), bf),
            pltpu.VMEM((slots, width), bf),
            pltpu.VMEM((slots, width), bf),
            pltpu.VMEM((MOST, BLK, width), jnp.float32),
            pltpu.VMEM((num_blocks, BLK, width), jnp.float32),
            pltpu.VMEM((n, tl, width), bf),
            pltpu.VMEM((n, tl, width), bf),
            pltpu.VMEM((n, tl, width), bf),
            pltpu.VMEM((n, tl, width), bf),
            dma((2 * MOST * hid,)), dma((2 * MOST * hid,)), dma((MOST,)), dma((MOST,)),
            dma((n,)), dma((n,)), dma((n,)), dma((n,)),
        ],
        compiler_params=pltpu.CompilerParams(
            collective_id=1, has_side_effects=True, vmem_limit_bytes=40 * 2**20),
    )(terms, factor, safe_slot)


def solution(mesh):
    return jax.shard_map(
        per_device,
        mesh=mesh,
        in_specs=(
            P("exp", ("sec", "hid")),
            P(("sec", "hid")),
            P("exp", None),
            P(),
            P("sec", None, ("exp", "hid")),
            P("sec", None, ("exp", "hid")),
            P("sec", ("exp", "hid"), None),
        ),
        out_specs=P("exp", ("sec", "hid")),
        check_vma=False,
    )
```

```python
import functools

import jax
import jax.numpy as jnp
from jax import lax
from jax.experimental import pallas as pl
from jax.experimental.pallas import tpu as pltpu
from jax.sharding import PartitionSpec as P

EXPERTS = 8
BLK = 128
MOST = 4
MESH = pl.DeviceIdType.MESH
EXTRA = 16


def greet(n, hid):
    e, s, h = lax.axis_index("exp"), lax.axis_index("sec"), lax.axis_index("hid")
    i, par = e // 2, e % 2
    barrier = pltpu.get_barrier_semaphore()
    for k in range(1, n):
        peer = lax.rem(i + k, n) * 2 + par
        pl.semaphore_signal(barrier, inc=1, device_id={"exp": peer}, device_id_type=MESH)
    pl.semaphore_signal(barrier, inc=1, device_id={"exp": i * 2 + 1 - par}, device_id_type=MESH)
    pl.semaphore_signal(barrier, inc=1, device_id={"sec": 1 - s}, device_id_type=MESH)
    for k in range(1, hid):
        pl.semaphore_signal(barrier, inc=1, device_id={"hid": lax.rem(h + k, hid)}, device_id_type=MESH)
    pl.semaphore_wait(barrier, (n - 1) + 1 + 1 + (hid - 1))
    return e, i, par, s, h


def remote(src, dst, sems, where, device):
    return pltpu.make_async_remote_copy(
        src_ref=src, dst_ref=dst, send_sem=sems[0].at[where], recv_sem=sems[1].at[where],
        device_id=device, device_id_type=MESH,
    )


def gather_kernel(n, hid, chunks, tok_ref, gain_ref, rw_ref, bos_ref, out_ref, rw_out, full, gw, *rest):
    gathered = rest[:chunks]
    zs, zr, xs, xr, ys, yr, hs, hr, gs, gr, ws, wr, vs, vr = rest[chunks:]
    e, i, par, s, h = greet(n, hid)
    tl = tok_ref.shape[0]
    half = full.shape[2]
    slots = MOST * BLK
    groups = full.shape[0]
    pair = {"exp": i * 2 + 1 - par}
    me = s * hid + h
    over = (1 - s) * hid + h
    parts = [pl.ds(k * BLK, BLK) for k in range(MOST)]
    parts[-1] = pl.ds((MOST - 1) * BLK, BLK + EXTRA)
    far, near, side, passed = {}, {}, {}, []

    def rows_of(c, index):
        return gathered[c].at[index * tl // BLK, pl.ds(pl.multiple_of(lax.rem(index * tl, BLK), tl), tl), :]

    def start(c):
        mine = rows_of(c, e)
        mine[...] = tok_ref[:, c * half:(c + 1) * half]
        for k in range(1, n):
            far[c, k] = remote(mine, mine, (zs, zr), c * n + k, {"exp": lax.rem(i + k, n) * 2 + par})
            far[c, k].start()
        near[c, 0] = remote(mine, mine, (xs, xr), c * n, pair)
        near[c, 0].start()

    def forward(c):
        for k in range(1, n):
            far[c, k].wait_recv()
            got = rows_of(c, lax.rem(i - k + n, n) * 2 + par)
            near[c, k] = remote(got, got, (xs, xr), c * n + k, pair)
            near[c, k].start()

    def pick(c):
        for k in range(n):
            near[c, k].wait_recv()
        spot = me * chunks + c
        full[spot, slots:, :] = jnp.broadcast_to(gain_ref[:, c * half:(c + 1) * half], (EXTRA, half))
        for k in range(MOST):
            full[spot, k * BLK:(k + 1) * BLK, :] = gathered[c][bos_ref[k]]
            ref = full.at[spot, parts[k], :]
            at = c * MOST + k
            side[c, k] = remote(ref, ref, (ys, yr), at, {"sec": 1 - s})
            side[c, k].start()
            for q in range(1, hid):
                copy = remote(ref, ref, (hs, hr), at * hid + q, {"hid": lax.rem(h + q, hid)})
                copy.start()
                passed.append(copy)

    def share(c):
        for k in range(MOST):
            side[c, k].wait_recv()
            ref = full.at[over * chunks + c, parts[k], :]
            for q in range(1, hid):
                copy = remote(ref, ref, (gs, gr), (c * MOST + k) * hid + q, {"hid": lax.rem(h + q, hid)})
                copy.start()
                passed.append(copy)

    gw[e] = rw_ref[...]
    wfar, wnear = [], [remote(gw.at[e], gw.at[e], (vs, vr), 0, pair)]
    start(0)
    for k in range(1, n):
        copy = remote(gw.at[e], gw.at[e], (ws, wr), k, {"exp": lax.rem(i + k, n) * 2 + par})
        copy.start()
        wfar.append(copy)
    wnear[0].start()
    for t in range(chunks + 2):
        if 0 <= t - 2:
            share(t - 2)
        if 0 <= t - 1 < chunks:
            pick(t - 1)
        if t < chunks:
            forward(t)
        if t + 1 < chunks:
            start(t + 1)
    for k in range(1, n):
        wfar[k - 1].wait_recv()
        got = gw.at[lax.rem(i - k + n, n) * 2 + par]
        copy = remote(got, got, (vs, vr), k, pair)
        copy.start()
        wnear.append(copy)
    for copy in passed:
        copy.wait_recv()

    def norm(step, carry):
        rows = pl.ds(pl.multiple_of(step * 32, 32), 32)
        total = jnp.zeros((32, 1), jnp.float32)
        for j in range(groups):
            v = full[j, rows, :].astype(jnp.float32)
            total = total + jnp.sum(v * v, axis=1, keepdims=True)
        rms = jnp.sqrt(total / (groups * half) + 1e-05)
        for j in range(groups):
            v = full[j, rows, :].astype(jnp.float32)
            gain = full[j, slots:slots + EXTRA, :].astype(jnp.float32)[0:1, :]
            out_ref[rows, j * half:(j + 1) * half] = (v * gain / rms).astype(out_ref.dtype)
        return carry

    lax.fori_loop(0, slots // 32, norm, 0)
    for copy in wnear:
        copy.wait_recv()
    rw_out[...] = gw[...]
    for copy in list(far.values()) + list(near.values()) + list(side.values()) + passed + wfar + wnear:
        copy.wait_send()


def ffn_kernel(first, tile, x_ref, gate_ref, up_ref, down_ref, out_ref, act):
    j = pl.program_id(0)

    @pl.when(j < first)
    def _():
        x = x_ref[...]
        gate = jnp.dot(x, gate_ref[0], preferred_element_type=jnp.float32)
        up = jnp.dot(x, up_ref[0], preferred_element_type=jnp.float32)
        vals = gate / (1.0 + jnp.exp(-gate)) * up
        act[:, pl.ds(pl.multiple_of(j * tile, tile), tile)] = vals.astype(act.dtype)

    @pl.when(j >= first)
    def _():
        out_ref[...] = jnp.dot(act[...], down_ref[0], preferred_element_type=jnp.float32).astype(out_ref.dtype)


def reduce_kernel(n, hid, chunks, term_ref, fac_ref, slot_ref, out_ref, hbuf, ysend, ybuf, spread,
                  psend, pbuf, qsend, qbuf, *rest):
    red = rest[:chunks]
    hs, hr, ys, yr, xs, xr, zs, zr = rest[chunks:]
    e, i, par, s, h = greet(n, hid)
    tl, width = out_ref.shape
    half = width // chunks
    order = [k for k in range(1, n)] + [0]
    pair = {"exp": i * 2 + 1 - par}
    first, across, near, far, own = {}, {}, {}, {}, {}

    def cols(side, at, c):
        sec = (1 - s) if side == 0 else s
        return pl.ds(pl.multiple_of((sec * hid + at) * width + c * half, half), half)

    def swap(c):
        for side in range(2):
            for q in range(1, hid):
                at = lax.rem(h + q, hid)
                first[c, side, q] = remote(
                    term_ref.at[:, cols(side, at, c)], hbuf.at[c * 2 + side, q], (hs, hr),
                    (c * 2 + side) * hid + q, {"hid": at})
                first[c, side, q].start()

    def cross(c):
        for side in range(2):
            for q in range(1, hid):
                first[c, side, q].wait_recv()
            for k in range(MOST):
                rows = pl.ds(k * BLK, BLK)
                total = term_ref[rows, cols(side, h, c)].astype(jnp.float32)
                for q in range(1, hid):
                    total = total + hbuf[c * 2 + side, q, rows, :].astype(jnp.float32)
                if side == 0:
                    ysend[c, rows, :] = total.astype(ysend.dtype)
                else:
                    red[c][k] = total
            if side == 0:
                across[c] = remote(ysend.at[c], ybuf.at[c], (ys, yr), c, {"sec": 1 - s})
                across[c].start()

    def part(c, dest):
        return spread[c, dest * tl // BLK, pl.ds(pl.multiple_of(lax.rem(dest * tl, BLK), tl), tl), :]

    def weigh(c):
        across[c].wait_recv()
        for k in range(MOST):
            red[c][k] = red[c][k] + ybuf[c, k * BLK:(k + 1) * BLK, :].astype(jnp.float32)
        for b in range(spread.shape[1]):
            spread[c, b] = red[c][slot_ref[b]] * fac_ref[b * BLK:(b + 1) * BLK, :]
        for k in order:
            at = c * n + k
            psend[at] = part(c, lax.rem(i + k, n) * 2 + 1 - par).astype(psend.dtype)
            near[c, k] = remote(psend.at[at], pbuf.at[at], (xs, xr), at, pair)
            near[c, k].start()

    def deliver(c):
        for k in order:
            at = c * n + k
            dest = lax.rem(i + k, n) * 2 + par
            near[c, k].wait_recv()
            mine = part(c, dest) + pbuf[at].astype(jnp.float32)
            if k:
                qsend[at] = mine.astype(qsend.dtype)
                far[c, k] = remote(qsend.at[at], qbuf.at[at], (zs, zr), at, {"exp": dest})
                far[c, k].start()
            else:
                own[c] = mine

    for c in range(chunks):
        swap(c)
    cross(0)
    for t in range(chunks + 1):
        if t + 1 < chunks:
            cross(t + 1)
        if t < chunks:
            weigh(t)
        if t >= 1:
            deliver(t - 1)
    for c in range(chunks):
        total = own[c]
        for k in range(1, n):
            far[c, k].wait_recv()
            total = total + qbuf[c * n + k].astype(jnp.float32)
        out_ref[:, c * half:(c + 1) * half] = total.astype(out_ref.dtype)
    for group in (first, across, near, far):
        for copy in group.values():
            copy.wait_send()


def per_device(tokens, norm_gain, route_weight, block_experts, w_gate, w_up, w_down):
    exp_devices = lax.axis_size("exp")
    hid = lax.axis_size("hid")
    n = exp_devices // 2
    group_size = exp_devices // EXPERTS
    my_expert = lax.axis_index("exp") // group_size
    tl, width = tokens.shape
    total_rows = tl * exp_devices
    num_blocks = total_rows // BLK
    slots = MOST * BLK
    model = w_gate.shape[1]
    hit = jnp.any(block_experts == my_expert, axis=1)
    ids = jnp.arange(num_blocks, dtype=jnp.int32)
    earlier = (ids[None, :] < ids[:, None]) & hit[None, :]
    slot_of_block = jnp.sum(earlier.astype(jnp.int32), axis=1)
    match = hit[None, :] & (slot_of_block[None, :] == jnp.arange(MOST, dtype=jnp.int32)[:, None])
    block_of_slot = jnp.sum(jnp.where(match, ids[None, :], 0), axis=1).astype(jnp.int32)
    safe_slot = jnp.where(hit, slot_of_block, 0).astype(jnp.int32)

    vmem = pl.BlockSpec(memory_space=pltpu.VMEM)
    smem = pl.BlockSpec(memory_space=pltpu.SMEM)
    dma = pltpu.SemaphoreType.DMA
    bf = jnp.bfloat16
    chunks = next(c for c in (4, 2, 1) if width % (c * BLK) == 0)
    half = width // chunks
    lanes = max(BLK, tl)
    packed = jnp.zeros((8, lanes), jnp.float32).at[:route_weight.shape[1], :tl].set(route_weight.T)
    normed, weights = pl.pallas_call(
        functools.partial(gather_kernel, n, hid, chunks),
        out_shape=(
            jax.ShapeDtypeStruct((slots, model), bf),
            jax.ShapeDtypeStruct((exp_devices, 8, lanes), jnp.float32),
        ),
        in_specs=[vmem, vmem, vmem, smem],
        out_specs=(vmem, vmem),
        scratch_shapes=[
            pltpu.VMEM((2 * hid * chunks, slots + EXTRA, half), bf),
            pltpu.VMEM((exp_devices, 8, lanes), jnp.float32),
            *[pltpu.VMEM((num_blocks, BLK, half), bf)] * chunks,
            *[dma((chunks * n,))] * 4,
            *[dma((chunks * MOST,))] * 2,
            *[dma((chunks * MOST * hid,))] * 4,
            *[dma((n,))] * 4,
        ],
        compiler_params=pltpu.CompilerParams(
            collective_id=0, has_side_effects=True, vmem_limit_bytes=32 * 2**20),
    )(tokens, norm_gain.reshape(1, width), packed, block_of_slot)

    weights = weights[:, :route_weight.shape[1], :tl].transpose(0, 2, 1).reshape(total_rows, -1)
    chosen = jnp.repeat(block_experts == my_expert, BLK, axis=0)
    factor = jnp.sum(jnp.where(chosen, weights, 0.0), axis=1, keepdims=True)

    units = w_gate.shape[2]
    tile = min(256, units)
    first = units // tile
    out_tile = min(512, model)
    flops = 6 * slots * model * units
    terms = pl.pallas_call(
        functools.partial(ffn_kernel, first, tile),
        grid=(first + model // out_tile,),
        out_shape=jax.ShapeDtypeStruct((slots, model), bf),
        in_specs=[
            pl.BlockSpec((slots, model), lambda j: (0, 0)),
            pl.BlockSpec((1, model, tile), lambda j: (0, 0, jnp.minimum(j, first - 1))),
            pl.BlockSpec((1, model, tile), lambda j: (0, 0, jnp.minimum(j, first - 1))),
            pl.BlockSpec((1, units, out_tile), lambda j: (0, 0, jnp.maximum(j - first, 0))),
        ],
        out_specs=pl.BlockSpec((slots, out_tile), lambda j: (0, jnp.maximum(j - first, 0))),
        scratch_shapes=[pltpu.VMEM((slots, units), bf)],
        compiler_params=pltpu.CompilerParams(vmem_limit_bytes=40 * 2**20),
        cost_estimate=pl.CostEstimate(
            flops=flops, bytes_accessed=6 * model * units, transcendentals=slots * units),
    )(normed, w_gate, w_up, w_down)

    return pl.pallas_call(
        functools.partial(reduce_kernel, n, hid, chunks),
        out_shape=jax.ShapeDtypeStruct((tl, width), bf),
        in_specs=[vmem, vmem, smem],
        out_specs=vmem,
        scratch_shapes=[
            pltpu.VMEM((2 * chunks, hid, slots, half), bf),
            *[pltpu.VMEM((chunks, slots, half), bf)] * 2,
            pltpu.VMEM((chunks, num_blocks, BLK, half), jnp.float32),
            *[pltpu.VMEM((chunks * n, tl, half), bf)] * 4,
            *[pltpu.VMEM((MOST, BLK, half), jnp.float32)] * chunks,
            *[dma((2 * chunks * hid,))] * 2,
            *[dma((chunks,))] * 2,
            *[dma((chunks * n,))] * 4,
        ],
        compiler_params=pltpu.CompilerParams(
            collective_id=1, has_side_effects=True, vmem_limit_bytes=40 * 2**20),
    )(terms, factor, safe_slot)


def solution(mesh):
    return jax.shard_map(
        per_device,
        mesh=mesh,
        in_specs=(
            P("exp", ("sec", "hid")),
            P(("sec", "hid")),
            P("exp", None),
            P(),
            P("sec", None, ("exp", "hid")),
            P("sec", None, ("exp", "hid")),
            P("sec", ("exp", "hid"), None),
        ),
        out_specs=P("exp", ("sec", "hid")),
        check_vma=False,
    )
```
